32 devices in a mesh: mesh: 8 (over z, y), comb: 4 (over x, core).
Axes of the slice: x: 2, y: 2, z: 4, core: 2. Of those that a mesh axis runs over, the one named last changes fastest.
Arguments:
- coeffs: bfloat16 [1024, 512], P('comb'), may hold values from -3 to 3
- basis: bfloat16 [3, 4096, 512], P(None, 'mesh', 'comb'), may hold values from -0.25 to 0.25
- connect: int32 [32, 4, 128], P('mesh'), may hold values from 0 to 767
- stiffness: float32 [32, 128], P('mesh'), may hold values from 0.3 to 3
- send_lists: int32 [8, 2, 128], P('mesh'), may hold values from 0 to 511, as said below
- elem_count: int32 [8], P('mesh'), may hold values from 128 to 512, as said below
Outputs:
- modal_force: float32 [1024, 512], P('comb', 'mesh')
The draws below stay inside these ranges and needn't reach their ends.
Inputs may be any that keep to these rules, and one draw needn't show every extreme that they name: `connect`: slots below 512 are the partition's own nodes, then 128 slots lent by the lower neighbour and 128 lent by the upper one; entries of element slots that are not live are arbitrary valid slots. `send_lists`: the 128 entries of each row are distinct local node numbers. `elem_count`: some partition is full and some holds a quarter of 512.
All inputs are finite; a program needn't handle non-finite values.
Results may differ from the reference program's by a relative error of at most 0.00071.
Values may be sent and summed in bfloat16 or wider, within the bound.
A program may use at most 64 MiB of HBM per device.

```python
import math
import jax
import jax.numpy as jnp
from jax import lax

M = 512
COMB_DEV = 256
NODE_DEV = 512
GHOST = 128
EBLK = 4
ELEM_CAP = 512
ELEM_BLOCKS = 32
COMBOS = 1024
NODES = 4096
N_MESH = 8
N_COMB = 4


def pick_lent(one_key):
    return jax.random.permutation(one_key, NODE_DEV)[:GHOST]


def draw_send_lists(key, part):
    key = jax.random.fold_in(key, 11)
    keyset = jax.random.split(key, N_MESH * 2)
    chosen = jax.vmap(pick_lent)(keyset)
    return chosen.reshape(N_MESH, 2, GHOST).astype(jnp.int32)


def draw_elem_count(key, part):
    key = jax.random.fold_in(key, 12)
    key_one, key_two, key_three = jax.random.split(key, 3)
    counts = jax.random.randint(key_one, (N_MESH,), ELEM_CAP // 4, ELEM_CAP + 1)
    fullest = jax.random.randint(key_two, (), 0, N_MESH)
    offset = jax.random.randint(key_three, (), 1, N_MESH)
    counts = counts.at[fullest].set(ELEM_CAP)
    counts = counts.at[(fullest + offset) % N_MESH].set(ELEM_CAP // 4)
    return counts.astype(jnp.int32)


def with_ends(result, key, low, high):
    shape = result.shape
    spot = [jax.random.randint(jax.random.fold_in(key, axis), (), 0, shape[axis]) for axis in range(len(shape))]
    result = result.at[tuple(spot)].set(low)
    longest = shape.index(max(shape))
    spot[longest] = (spot[longest] + 1) % shape[longest]
    return result.at[tuple(spot)].set(high)


def levels(stream_key, extent, pieces, least, high):
    def one(axis_at, blocks):
        heights = jax.random.uniform(jax.random.fold_in(jax.random.fold_in(stream_key, 6), axis_at), (blocks,), jnp.float32, least / len(pieces), high / len(pieces))
        return jnp.repeat(jnp.exp(heights), extent[axis_at] // blocks).reshape((-1,) + (1,) * (len(extent) - axis_at - 1))

    factor_of = one(*pieces[0])
    for cut in pieces[1:]:
        factor_of = factor_of * one(*cut)
    return factor_of


def gaussian(rng, dims, scale, bound, pieces=(), held_as=jnp.bfloat16):
    drawn = jax.random.normal(rng, dims, jnp.float32) * scale
    if len(pieces) > 0:
        drawn = levels(rng, dims, pieces, -0.22, 0.18) * drawn
    return jnp.clip(drawn, min=-bound, max=bound).astype(held_as)


def setup_inputs(seed: int = 0) -> dict:
    streams_of = jax.random.split(jax.random.key(seed), 7)
    coeffs = gaussian(streams_of[0], (COMBOS, M), 0.5, 3.0, ((0, 4),))
    basis = gaussian(streams_of[1], (3, NODES, M), M ** -0.5, 0.25, ((1, 8), (2, 4)))
    connect = with_ends(jax.random.randint(streams_of[2], (ELEM_BLOCKS, 4, 128), 0, NODE_DEV + 2 * GHOST), jax.random.fold_in(streams_of[2], 1), 0, (NODE_DEV + 2 * GHOST) - 1).astype(jnp.int32)
    stiffness = jnp.clip(jnp.exp(math.log(3.0) - 2.3025851 * jax.random.uniform(streams_of[3], (ELEM_BLOCKS, 128), jnp.float32) ** levels(streams_of[3], (ELEM_BLOCKS, 128), ((0, 8),), -0.2, 0.2)), 0.3, 3.0)
    send_lists = draw_send_lists(jax.random.fold_in(streams_of[6], 71), 0)
    elem_count = draw_elem_count(jax.random.fold_in(streams_of[6], 71), 0)
    return dict(coeffs=coeffs, basis=basis, connect=connect, stiffness=stiffness, send_lists=send_lists, elem_count=elem_count)


stiff_cubic = 0.3
twist_ratio = 0.5


def spring_pull(start_node, end_node, stiff_now):
    stretch = end_node - start_node
    factor = stiff_now * (1.0 + stiff_cubic * jnp.sum(stretch * stretch, axis=0, keepdims=True))
    return factor * stretch


def element_forces(corners, stiff_now):
    points = [corners[..., 0, :], corners[..., 1, :], corners[..., 2, :], corners[..., 3, :]]
    totals = [jnp.zeros_like(points[0]) for unused in range(4)]
    edge_pairs = [(0, 1), (1, 2), (2, 3), (3, 0), (0, 2), (1, 3)]
    for lower_end, upper_end in edge_pairs:
        tension = spring_pull(points[lower_end], points[upper_end], stiff_now)
        totals[upper_end] = totals[upper_end] + tension
        totals[lower_end] = totals[lower_end] - tension
    twist = twist_ratio * stiff_now * (points[0] - points[1] + points[2] - points[3])
    totals[0] = totals[0] + twist
    totals[1] = totals[1] - twist
    totals[2] = totals[2] + twist
    totals[3] = totals[3] - twist
    return jnp.stack(totals, axis=-2)


def reference(coeffs, basis, connect, stiffness, send_lists, elem_count):
    sentinel = N_MESH * NODE_DEV
    part_ids = jnp.arange(N_MESH, dtype=jnp.int32)
    own_slots = part_ids[:, None] * NODE_DEV + jnp.arange(NODE_DEV, dtype=jnp.int32)[None, :]
    from_lower = jnp.roll(send_lists[:, 1, :], 1, axis=0) + ((part_ids - 1) * NODE_DEV)[:, None]
    from_lower = jnp.where((part_ids > 0)[:, None], from_lower, sentinel)
    from_upper = jnp.roll(send_lists[:, 0, :], -1, axis=0) + ((part_ids + 1) * NODE_DEV)[:, None]
    from_upper = jnp.where((part_ids < N_MESH - 1)[:, None], from_upper, sentinel)
    slot_map = jnp.concatenate([own_slots, from_lower, from_upper], axis=1).astype(jnp.int32)
    basis_real = basis.astype(jnp.float32)
    basis_wide = jnp.concatenate([basis_real, jnp.zeros((3, 1, M), jnp.float32)], axis=1)
    blocks = connect.reshape(N_MESH, EBLK, 4, 128)
    element_ids = jnp.arange(EBLK * 128, dtype=jnp.int32).reshape(EBLK, 128)
    live_mask = element_ids[None, :, :] < elem_count[:, None, None]
    stiff_live = jnp.where(live_mask, stiffness.reshape(N_MESH, EBLK, 128), jnp.float32(0.0))
    out_scale = (M / (3.0 * N_MESH * NODE_DEV)) ** 0.5
    slot_width = NODE_DEV + 2 * GHOST

    def one_group(group_coeffs):
        displaced = jnp.einsum("cm,dnm->dcn", group_coeffs.astype(jnp.float32), basis_real).astype(jnp.bfloat16)
        displaced = jnp.concatenate([displaced, jnp.zeros((3, COMB_DEV, 1), displaced.dtype)], axis=2)

        def one_part(total, inputs):
            slots, part_conn, part_stiff = inputs
            local_disp = displaced[:, :, slots]
            flat_slots = part_conn.reshape(-1)
            corners = local_disp[:, :, flat_slots].astype(jnp.float32).reshape(3, COMB_DEV, EBLK, 4, 128)
            pushed = element_forces(corners, part_stiff)
            nodal_force = jnp.zeros((3, COMB_DEV, slot_width), jnp.float32)
            nodal_force = nodal_force.at[:, :, flat_slots].add(pushed.reshape(3, COMB_DEV, EBLK * 512))
            nodal_force = nodal_force.astype(jnp.bfloat16)
            rows_here = basis_wide[:, slots, :]
            total = total + jnp.einsum("dcn,dnm->cm", nodal_force.astype(jnp.float32), rows_here)
            return total, None

        total, unused = lax.scan(one_part, jnp.zeros((COMB_DEV, M), jnp.float32), (slot_map, blocks, stiff_live))
        return total * out_scale

    results = lax.map(one_group, coeffs.reshape(N_COMB, COMB_DEV, M))
    return results.reshape(N_COMB * COMB_DEV, M)
```

```python
import functools

import jax
import jax.numpy as jnp
from jax import lax
from jax.experimental import pallas as pl
from jax.experimental.pallas import tpu as pltpu
from jax.sharding import PartitionSpec as P

stiff_cubic = 0.3
twist_ratio = 0.5
MESH = pl.DeviceIdType.MESH


def with_halo(shard, sides, width):
    for axis, dim in sides:
        size, length = (lax.axis_size(axis), shard.shape[dim])
        up = [(i, (i + 1) % size) for i in range(size - 1)]
        down = [(j, i) for i, j in up]
        last = lax.slice_in_dim(shard, length - width, length, axis=dim)
        leading = lax.slice_in_dim(shard, 0, width, axis=dim)
        before = lax.ppermute(last, axis, up)
        after = lax.ppermute(leading, axis, down)
        shard = jnp.concatenate([before, shard, after], axis=dim)
    return shard


def spring_pull(start_node, end_node, stiff_now):
    stretch = end_node - start_node
    factor = stiff_now * (1.0 + stiff_cubic * jnp.sum(stretch * stretch, axis=1, keepdims=True))
    return factor * stretch


def element_forces(corners, stiff_now):
    points = [corners[0], corners[1], corners[2], corners[3]]
    totals = [jnp.zeros_like(points[0]) for unused in range(4)]
    edge_pairs = [(0, 1), (1, 2), (2, 3), (3, 0), (0, 2), (1, 3)]
    for lower_end, upper_end in edge_pairs:
        tension = spring_pull(points[lower_end], points[upper_end], stiff_now)
        totals[upper_end] = totals[upper_end] + tension
        totals[lower_end] = totals[lower_end] - tension
    twist = twist_ratio * stiff_now * (points[0] - points[1] + points[2] - points[3])
    totals[0] = totals[0] + twist
    totals[1] = totals[1] - twist
    totals[2] = totals[2] + twist
    totals[3] = totals[3] - twist
    return jnp.stack(totals, axis=0)


def body(coeffs, basis, connect, stiffness, send_lists, elem_count):
    node_rows = basis.shape[1]
    ghost_rows = send_lists.shape[2]
    comb_rows = coeffs.shape[0]
    chosen = send_lists[0]
    whole_basis = lax.all_gather(basis, "comb", axis=2, tiled=True)
    displaced = jnp.einsum(
        "cm,dnm->ndc", coeffs, whole_basis, preferred_element_type=jnp.float32
    ).astype(jnp.bfloat16)
    rim_disp = displaced[chosen]
    disp_halo = with_halo(rim_disp, (("mesh", 0),), 1)
    displaced = jnp.concatenate([displaced, disp_halo[0], disp_halo[3]], axis=0)
    slot_width = displaced.shape[0]
    lane_ids = jnp.arange(128, dtype=jnp.int32)
    live_count = elem_count[0]

    def add_block(block_id, forces):
        slot_ids = lax.dynamic_index_in_dim(connect, block_id, 0, keepdims=False).reshape(-1)
        stiff_now = lax.dynamic_index_in_dim(stiffness, block_id, 0, keepdims=False)
        stiff_now = jnp.where(block_id * 128 + lane_ids < live_count, stiff_now, jnp.float32(0.0))
        corners = (
            jnp.take(displaced, slot_ids, axis=0).astype(jnp.float32).reshape(4, 128, 3, comb_rows)
        )
        pushed = element_forces(corners, stiff_now[:, None, None])
        return forces.at[slot_ids].add(pushed.reshape(512, 3, comb_rows))

    forces = lax.fori_loop(
        0, (live_count + 127) // 128, add_block, jnp.zeros((slot_width, 3, comb_rows), jnp.float32)
    )
    nodal_force = forces.astype(jnp.bfloat16)
    modal = jnp.einsum(
        "ndc,dnm->cm", nodal_force[:node_rows], whole_basis, preferred_element_type=jnp.float32
    )
    borrowed = nodal_force[node_rows:].reshape(2, ghost_rows, 3, comb_rows)
    returned = with_halo(borrowed, (("mesh", 0),), 1)
    back_rows = jnp.stack([returned[0], returned[3]], axis=0)
    modal = modal + jnp.einsum(
        "kgdc,dkgm->cm", back_rows, whole_basis[:, chosen, :], preferred_element_type=jnp.float32
    )
    out_scale = (whole_basis.shape[2] / (3.0 * node_rows * lax.axis_size("mesh"))) ** 0.5
    return lax.psum_scatter(modal * out_scale, "mesh", scatter_dimension=1, tiled=True)


def fused_kernel(n_mesh, coeffs_ref, basis_ref, connect_ref, stiff_ref, send_ref, count_ref, out_ref,
                 coef_s, wide, inc, lent_onehot, lent_own, lent_far, disp_v, force_s, modal_acc,
                 part_out, part_in,
                 s_mate, r_mate, s_far, r_far, s_fwd, r_fwd, s_lent, r_lent, s_rim, r_rim,
                 s_part, r_part):
    p = lax.axis_index("mesh")
    q = lax.axis_index("comb")
    core = lax.rem(q, 2)
    chip = q // 2
    mate = q + 1 - 2 * core
    far = lax.rem(q + 2, 4)
    lane_own = pl.multiple_of((core * 2 + chip) * 128, 128)
    lane_far = pl.multiple_of((core * 2 + 1 - chip) * 128, 128)
    lane_half = pl.multiple_of(core * 256, 256)
    has_low = p > 0
    has_up = p < n_mesh - 1
    nodes = basis_ref.shape[1]
    ghost = send_ref.shape[1]

    def remote(src, dst, ssem, rsem, pp, qq):
        return pltpu.make_async_remote_copy(
            src_ref=src, dst_ref=dst, send_sem=ssem, recv_sem=rsem,
            device_id=(pp, qq), device_id_type=MESH)

    barrier = pltpu.get_barrier_semaphore()
    pl.semaphore_signal(barrier, inc=1, device_id=(p, mate), device_id_type=MESH)
    pl.semaphore_signal(barrier, inc=1, device_id=(p, far), device_id_type=MESH)
    for r in range(1, n_mesh):
        pl.semaphore_signal(barrier, inc=1, device_id=(lax.rem(p + r, n_mesh), q), device_id_type=MESH)

    for at, blk in enumerate((0, 2, 1, 3)):
        coef_s[:, at * 128:(at + 1) * 128] = coeffs_ref[:, blk * 128:(blk + 1) * 128]
    for side in range(2):
        ids = jnp.broadcast_to(send_ref[side:side + 1, :].astype(jnp.float32), (ghost, ghost)).T
        for at in range(nodes // 128):
            lanes = (lax.broadcasted_iota(jnp.int32, (ghost, 128), 1) + at * 128).astype(jnp.float32)
            lent_onehot[side * ghost:(side + 1) * ghost, at * 128:(at + 1) * 128] = jnp.where(
                ids == lanes, 1.0, 0.0).astype(jnp.bfloat16)

    pl.semaphore_wait(barrier, n_mesh + 1)

    own = pl.ds(0, nodes)
    rim = pl.ds(nodes, 2 * ghost)

    def far_copy(d):
        return remote(basis_ref.at[d], wide.at[d, own, pl.ds(lane_own, 128)], s_far.at[d], r_far.at[d], p, far)

    def mate_copy(d):
        return remote(basis_ref.at[d], wide.at[d, own, pl.ds(lane_own, 128)], s_mate.at[d], r_mate.at[d], p, mate)

    def fwd_copy(d):
        src = wide.at[d, own, pl.ds(lane_far, 128)]
        return remote(src, src, s_fwd.at[d], r_fwd.at[d], p, mate)

    def rim_copy(d):
        src = wide.at[d, rim, pl.ds(lane_half, 256)]
        return remote(src, src, s_rim.at[d], r_rim.at[d], p, mate)

    def lent_copy(kind, d, side):
        src = (lent_own if kind == 0 else lent_far).at[d, pl.ds(side * ghost, ghost)]
        slot = nodes + ghost if side == 0 else nodes
        lane = lane_own if kind == 0 else lane_far
        dst = wide.at[d, pl.ds(slot, ghost), pl.ds(lane, 128)]
        to = p - 1 if side == 0 else p + 1
        return remote(src, dst, s_lent.at[kind, d, side], r_lent.at[kind, d, side], to, q)

    for d in range(3):
        far_copy(d).start()
    for d in range(3):
        mate_copy(d).start()

    def lend(kind, d):
        src = basis_ref[d] if kind == 0 else wide[d, :nodes, pl.ds(lane_far, 128)]
        rows = jnp.dot(lent_onehot[...], src, preferred_element_type=jnp.float32).astype(jnp.bfloat16)
        if kind == 0:
            lent_own[d] = rows
        else:
            lent_far[d] = rows

        @pl.when(has_low)
        def _():
            lent_copy(kind, d, 0).start()

        @pl.when(has_up)
        def _():
            lent_copy(kind, d, 1).start()

    for d in range(3):
        lend(0, d)
    for d in range(3):
        wide[d, :nodes, pl.ds(lane_own, 128)] = basis_ref[d]

    @pl.when(jnp.logical_not(has_low))
    def _():
        for d in range(3):
            wide[d, nodes:nodes + ghost, pl.ds(lane_half, 256)] = jnp.zeros((ghost, 256), jnp.bfloat16)

    @pl.when(jnp.logical_not(has_up))
    def _():
        for d in range(3):
            wide[d, nodes + ghost:, pl.ds(lane_half, 256)] = jnp.zeros((ghost, 256), jnp.bfloat16)

    elems = stiff_ref.shape[0] * 128

    def build(i, carry):
        rows = pl.ds(pl.multiple_of(i * 64, 64), 64)
        ids = lax.broadcasted_iota(jnp.int32, (64, 128), 0) + i * 64
        for b in range(elems // 128):
            base = jnp.where(ids == connect_ref[b, 0:1, :], 1.0, 0.0)
            for t in range(3):
                one = jnp.where(ids == connect_ref[b, t + 1:t + 2, :], 1.0, 0.0)
                inc[rows, t * elems + b * 128:t * elems + (b + 1) * 128] = (one - base).astype(jnp.bfloat16)
        return carry

    lax.fori_loop(0, wide.shape[1] // 64, build, 0)

    def stage_far(d):
        far_copy(d).wait_recv()
        fwd_copy(d).start()
        lend(1, d)

    def stage_rim(d):
        @pl.when(has_up)
        def _():
            lent_copy(0, d, 0).wait_recv()
            lent_copy(1, d, 0).wait_recv()

        @pl.when(has_low)
        def _():
            lent_copy(0, d, 1).wait_recv()
            lent_copy(1, d, 1).wait_recv()

        rim_copy(d).start()

    combos = coeffs_ref.shape[0]

    def stage_disp(d):
        mate_copy(d).wait_recv()
        fwd_copy(d).wait_recv()
        rim_copy(d).wait_recv()
        disp = lax.dot_general(coef_s[...], wide[d], (((1,), (1,)), ((), ())),
                               preferred_element_type=jnp.float32).astype(jnp.bfloat16)
        for t in range(3):
            disp_v[d * combos:(d + 1) * combos, t * elems:(t + 1) * elems] = jnp.dot(
                disp, inc[:, t * elems:(t + 1) * elems], preferred_element_type=jnp.float32)

    stage_far(0)
    stage_far(1)
    stage_rim(0)
    stage_disp(0)
    stage_far(2)
    stage_rim(1)
    stage_disp(1)
    stage_rim(2)
    stage_disp(2)

    count = count_ref[0]
    slots = wide.shape[1]
    modes = wide.shape[2]
    scale = (modes / (3.0 * nodes * n_mesh)) ** 0.5
    chunks = part_out.shape[0]
    crow = combos // chunks
    tile = 16

    for h in range(chunks):
        def tile_force(i, carry):
            for b in range(elems // 128):
                lane = lax.broadcasted_iota(jnp.int32, (1, 128), 1) + b * 128
                k = jnp.where(lane < count, stiff_ref[b:b + 1, :], 0.0)
                k3 = jnp.broadcast_to(k * stiff_cubic, (tile, 128))
                kt = jnp.broadcast_to(k * twist_ratio, (tile, 128))
                kb = jnp.broadcast_to(k, (tile, 128))

                def vec(t):
                    return [disp_v[pl.ds(pl.multiple_of(d * combos + h * crow + i * tile, tile), tile),
                                   t * elems + b * 128:t * elems + (b + 1) * 128] for d in range(3)]
                vb, vc, vd = vec(0), vec(1), vec(2)

                def dot3(x, y):
                    return x[0] * y[0] + x[1] * y[1] + x[2] * y[2]

                def sub3(x, y):
                    return [x[j] - y[j] for j in range(3)]

                def stiff(x):
                    return kb + k3 * dot3(x, x)
                bc, cd, bd = sub3(vc, vb), sub3(vd, vc), sub3(vd, vb)
                sab, sac, sad = stiff(vb), stiff(vc), stiff(vd)
                sbc, scd, sbd = stiff(bc), stiff(cd), stiff(bd)
                for d in range(3):
                    tw = kt * (vb[d] + cd[d])
                    tbc, tcd, tbd = sbc * bc[d], scd * cd[d], sbd * bd[d]
                    fb = sab * vb[d] - tbc - tbd + tw
                    fc = sac * vc[d] + tbc - tcd - tw
                    fd = sad * vd[d] + tcd + tbd + tw
                    for t, f in enumerate((fb, fc, fd)):
                        high = f.astype(jnp.bfloat16)
                        low = (f - high.astype(jnp.float32)).astype(jnp.bfloat16)
                        lanes = slice(t * elems + b * 128, t * elems + (b + 1) * 128)
                        force_s[pl.ds(pl.multiple_of(d * crow + i * tile, tile), tile), lanes] = high
                        force_s[pl.ds(pl.multiple_of((3 + d) * crow + i * tile, tile), tile), lanes] = low
            return carry

        lax.fori_loop(0, crow // tile, tile_force, 0)

        for g in range(slots // 256):
            rows = slice(g * 256, (g + 1) * 256)
            both = lax.dot_general(force_s[...], inc[rows, :], (((1,), (1,)), ((), ())),
                                   preferred_element_type=jnp.float32)
            nodal = (both[:3 * crow] + both[3 * crow:]).astype(jnp.bfloat16)
            add = jnp.dot(nodal[:crow], wide[0, rows, :], preferred_element_type=jnp.float32)
            for d in range(1, 3):
                add += jnp.dot(nodal[d * crow:(d + 1) * crow], wide[d, rows, :], preferred_element_type=jnp.float32)
            if g == 0:
                modal_acc[...] = add
            else:
                modal_acc[...] += add

        low_half = lax.broadcasted_iota(jnp.int32, (crow // 2, 128), 1) < 64
        for blk in range(4):
            at = ((blk % 2) * 2 + blk // 2) * 128
            top = modal_acc[:crow // 2, at:at + 128] * scale
            bottom = modal_acc[crow // 2:, at:at + 128] * scale
            part_out[h, 2 * blk] = jnp.where(low_half, top, pltpu.roll(bottom, 64, 1))
            part_out[h, 2 * blk + 1] = jnp.where(low_half, pltpu.roll(top, 64, 1), bottom)
        for r in range(1, n_mesh):
            part_copy(remote, part_out, part_in, s_part, r_part, h, r, p, q, n_mesh).start()

    for h in range(chunks):
        total = part_out[h, p]
        for r in range(1, n_mesh):
            part_copy(remote, part_out, part_in, s_part, r_part, h, r, p, q, n_mesh).wait_recv()
            total = total + part_in[h, r - 1]
        out_ref[h * crow:h * crow + crow // 2, :] = total[:, :64]
        out_ref[h * crow + crow // 2:(h + 1) * crow, :] = pltpu.roll(total, 64, 1)[:, :64]

    for d in range(3):
        far_copy(d).wait_send()
        mate_copy(d).wait_send()
        fwd_copy(d).wait_send()
        rim_copy(d).wait_send()
        for kind in range(2):
            @pl.when(has_low)
            def _():
                lent_copy(kind, d, 0).wait_send()

            @pl.when(has_up)
            def _():
                lent_copy(kind, d, 1).wait_send()
    for h in range(chunks):
        for r in range(1, n_mesh):
            part_copy(remote, part_out, part_in, s_part, r_part, h, r, p, q, n_mesh).wait_send()


def part_copy(remote, part_out, part_in, s_part, r_part, h, r, p, q, n_mesh):
    to = lax.rem(p + r, n_mesh)
    return remote(part_out.at[h, to], part_in.at[h, r - 1], s_part.at[h, r - 1], r_part.at[h, r - 1], to, q)


def fused_body(coeffs, basis, connect, stiffness, send_lists, elem_count):
    n_mesh = lax.axis_size("mesh")
    combos, modes = coeffs.shape
    nodes = basis.shape[1]
    ghost = send_lists.shape[2]
    slots = nodes + 2 * ghost
    elems = stiffness.shape[0] * 128
    chunks = 2
    crow = combos // chunks
    bf16, f32 = jnp.bfloat16, jnp.float32
    vmem = pl.BlockSpec(memory_space=pltpu.VMEM)
    dma = pltpu.SemaphoreType.DMA
    return pl.pallas_call(
        functools.partial(fused_kernel, n_mesh),
        out_shape=jax.ShapeDtypeStruct((combos, modes // n_mesh), f32),
        in_specs=[vmem] * 5 + [pl.BlockSpec(memory_space=pltpu.SMEM)],
        out_specs=vmem,
        scratch_shapes=[
            pltpu.VMEM((combos, modes), bf16),
            pltpu.VMEM((3, slots, modes), bf16),
            pltpu.VMEM((slots, 3 * elems), bf16),
            pltpu.VMEM((2 * ghost, nodes), bf16),
            pltpu.VMEM((3, 2 * ghost, 128), bf16),
            pltpu.VMEM((3, 2 * ghost, 128), bf16),
            pltpu.VMEM((3 * combos, 3 * elems), f32),
            pltpu.VMEM((6 * crow, 3 * elems), bf16),
            pltpu.VMEM((crow, modes), f32),
            pltpu.VMEM((chunks, n_mesh, crow // 2, 128), f32),
            pltpu.VMEM((chunks, n_mesh - 1, crow // 2, 128), f32),
            dma((3,)), dma((3,)), dma((3,)), dma((3,)), dma((3,)), dma((3,)),
            dma((2, 3, 2)), dma((2, 3, 2)), dma((3,)), dma((3,)),
            dma((chunks, n_mesh - 1)), dma((chunks, n_mesh - 1)),
        ],
        compiler_params=pltpu.CompilerParams(
            collective_id=0, has_side_effects=True, vmem_limit_bytes=48 * 2 ** 20),
        cost_estimate=pl.CostEstimate(flops=6 * 10 ** 9, bytes_accessed=4 * 10 ** 6, transcendentals=0),
    )(coeffs, basis, connect, stiffness, send_lists[0], elem_count)


def any_body(coeffs, basis, connect, stiffness, send_lists, elem_count):
    fits = (lax.axis_size("comb") == 4 and lax.axis_size("mesh") == 8 and coeffs.shape == (256, 512)
            and basis.shape == (3, 512, 128) and send_lists.shape[1:] == (2, 128) and stiffness.shape[0] == 4)
    return (fused_body if fits else body)(coeffs, basis, connect, stiffness, send_lists, elem_count)


def solution(mesh):
    in_specs = (
        P("comb", None),
        P(None, "mesh", "comb"),
        P("mesh", None, None),
        P("mesh", None),
        P("mesh", None, None),
        P("mesh"),
    )
    out_specs = P("comb", "mesh")
    return jax.shard_map(any_body, mesh=mesh, in_specs=in_specs, out_specs=out_specs, check_vma=False)
```

```python
import functools

import jax
import jax.numpy as jnp
from jax import lax
from jax.experimental import pallas as pl
from jax.experimental.pallas import tpu as pltpu
from jax.sharding import PartitionSpec as P

stiff_cubic = 0.3
twist_ratio = 0.5
MESH = pl.DeviceIdType.MESH


def with_halo(shard, sides, width):
    for axis, dim in sides:
        size, length = (lax.axis_size(axis), shard.shape[dim])
        up = [(i, (i + 1) % size) for i in range(size - 1)]
        down = [(j, i) for i, j in up]
        last = lax.slice_in_dim(shard, length - width, length, axis=dim)
        leading = lax.slice_in_dim(shard, 0, width, axis=dim)
        before = lax.ppermute(last, axis, up)
        after = lax.ppermute(leading, axis, down)
        shard = jnp.concatenate([before, shard, after], axis=dim)
    return shard


def spring_pull(start_node, end_node, stiff_now):
    stretch = end_node - start_node
    factor = stiff_now * (1.0 + stiff_cubic * jnp.sum(stretch * stretch, axis=1, keepdims=True))
    return factor * stretch


def element_forces(corners, stiff_now):
    points = [corners[0], corners[1], corners[2], corners[3]]
    totals = [jnp.zeros_like(points[0]) for unused in range(4)]
    edge_pairs = [(0, 1), (1, 2), (2, 3), (3, 0), (0, 2), (1, 3)]
    for lower_end, upper_end in edge_pairs:
        tension = spring_pull(points[lower_end], points[upper_end], stiff_now)
        totals[upper_end] = totals[upper_end] + tension
        totals[lower_end] = totals[lower_end] - tension
    twist = twist_ratio * stiff_now * (points[0] - points[1] + points[2] - points[3])
    totals[0] = totals[0] + twist
    totals[1] = totals[1] - twist
    totals[2] = totals[2] + twist
    totals[3] = totals[3] - twist
    return jnp.stack(totals, axis=0)


def body(coeffs, basis, connect, stiffness, send_lists, elem_count):
    node_rows = basis.shape[1]
    ghost_rows = send_lists.shape[2]
    comb_rows = coeffs.shape[0]
    chosen = send_lists[0]
    whole_basis = lax.all_gather(basis, "comb", axis=2, tiled=True)
    displaced = jnp.einsum(
        "cm,dnm->ndc", coeffs, whole_basis, preferred_element_type=jnp.float32
    ).astype(jnp.bfloat16)
    rim_disp = displaced[chosen]
    disp_halo = with_halo(rim_disp, (("mesh", 0),), 1)
    displaced = jnp.concatenate([displaced, disp_halo[0], disp_halo[3]], axis=0)
    slot_width = displaced.shape[0]
    lane_ids = jnp.arange(128, dtype=jnp.int32)
    live_count = elem_count[0]

    def add_block(block_id, forces):
        slot_ids = lax.dynamic_index_in_dim(connect, block_id, 0, keepdims=False).reshape(-1)
        stiff_now = lax.dynamic_index_in_dim(stiffness, block_id, 0, keepdims=False)
        stiff_now = jnp.where(block_id * 128 + lane_ids < live_count, stiff_now, jnp.float32(0.0))
        corners = (
            jnp.take(displaced, slot_ids, axis=0).astype(jnp.float32).reshape(4, 128, 3, comb_rows)
        )
        pushed = element_forces(corners, stiff_now[:, None, None])
        return forces.at[slot_ids].add(pushed.reshape(512, 3, comb_rows))

    forces = lax.fori_loop(
        0, (live_count + 127) // 128, add_block, jnp.zeros((slot_width, 3, comb_rows), jnp.float32)
    )
    nodal_force = forces.astype(jnp.bfloat16)
    modal = jnp.einsum(
        "ndc,dnm->cm", nodal_force[:node_rows], whole_basis, preferred_element_type=jnp.float32
    )
    borrowed = nodal_force[node_rows:].reshape(2, ghost_rows, 3, comb_rows)
    returned = with_halo(borrowed, (("mesh", 0),), 1)
    back_rows = jnp.stack([returned[0], returned[3]], axis=0)
    modal = modal + jnp.einsum(
        "kgdc,dkgm->cm", back_rows, whole_basis[:, chosen, :], preferred_element_type=jnp.float32
    )
    out_scale = (whole_basis.shape[2] / (3.0 * node_rows * lax.axis_size("mesh"))) ** 0.5
    return lax.psum_scatter(modal * out_scale, "mesh", scatter_dimension=1, tiled=True)


def fused_kernel(n_mesh, coeffs_any, basis_any, connect_any, stiff_any, send_any, count_ref, out_ref,
                 coeffs_ref, basis_ref, connect_ref, stiff_ref, send_ref, s_in, known,
                 coef_s, wide, inc, lent_onehot, lent_own, lent_far, disp_v, force_s, modal_acc,
                 disp_s, part_own, part_out, part_in,
                 s_mate, r_mate, s_far, r_far, s_fwd, r_fwd, s_lent, r_lent, s_rim, r_rim,
                 s_part, r_part):
    p = lax.axis_index("mesh")
    q = lax.axis_index("comb")
    core = lax.rem(q, 2)
    chip = q // 2
    mate = q + 1 - 2 * core
    far = lax.rem(q + 2, 4)
    lane_own = pl.multiple_of((core * 2 + chip) * 128, 128)
    lane_far = pl.multiple_of((core * 2 + 1 - chip) * 128, 128)
    lane_half = pl.multiple_of(core * 256, 256)
    has_low = p > 0
    has_up = p < n_mesh - 1
    nodes = basis_ref.shape[1]
    ghost = send_ref.shape[2]

    def remote(src, dst, ssem, rsem, pp, qq):
        return pltpu.make_async_remote_copy(
            src_ref=src, dst_ref=dst, send_sem=ssem, recv_sem=rsem,
            device_id=(pp, qq), device_id_type=MESH)

    y_mate = p + 1 - 2 * lax.rem(p, 2)
    has_z_low = p >= 2
    has_z_up = p < n_mesh - 2
    greets = 3 + jnp.where(has_z_low, 1, 0) + jnp.where(has_z_up, 1, 0)

    def greet(sem):
        pl.semaphore_signal(sem, inc=1, device_id=(p, mate), device_id_type=MESH)
        pl.semaphore_signal(sem, inc=1, device_id=(p, far), device_id_type=MESH)
        pl.semaphore_signal(sem, inc=1, device_id=(y_mate, q), device_id_type=MESH)

        @pl.when(has_z_low)
        def _():
            pl.semaphore_signal(sem, inc=1, device_id=(p - 2, q), device_id_type=MESH)

        @pl.when(has_z_up)
        def _():
            pl.semaphore_signal(sem, inc=1, device_id=(p + 2, q), device_id_type=MESH)

    barrier = pltpu.get_barrier_semaphore()
    greet(barrier)

    loads = [pltpu.make_async_copy(src, dst, s_in.at[n]) for n, (src, dst) in enumerate((
        (send_any, send_ref), (connect_any, connect_ref), (basis_any, basis_ref),
        (coeffs_any, coeffs_ref), (stiff_any, stiff_ref)))]
    for load in loads:
        load.start()
    own = pl.ds(0, nodes)
    rim = pl.ds(nodes, 2 * ghost)
    elems = stiff_ref.shape[0] * 128

    pl.semaphore_wait(barrier, greets)

    def far_copy(d):
        return remote(basis_any.at[d], wide.at[d, own, pl.ds(lane_own, 128)], s_far.at[d], r_far.at[d], p, far)

    def mate_copy(d):
        return remote(basis_any.at[d], wide.at[d, own, pl.ds(lane_own, 128)], s_mate.at[d], r_mate.at[d], p, mate)

    def fwd_copy(d):
        src = wide.at[d, own, pl.ds(lane_far, 128)]
        return remote(src, src, s_fwd.at[d], r_fwd.at[d], p, mate)

    def rim_copy(d):
        src = wide.at[d, rim, pl.ds(lane_half, 256)]
        return remote(src, src, s_rim.at[d], r_rim.at[d], p, mate)

    def lent_copy(kind, d, side):
        src = (lent_far if kind == 1 else lent_own).at[d, pl.ds(side * ghost, ghost)]
        slot = nodes + ghost if side == 0 else nodes
        lane = lane_far if kind == 1 else lane_own
        dst = wide.at[d, pl.ds(slot, ghost), pl.ds(lane, 128)]
        to = p - 1 if side == 0 else p + 1
        sem = min(kind, 1)
        return remote(src, dst, s_lent.at[sem, d, side], r_lent.at[sem, d, side], to, far if kind == 2 else q)

    def lend(kind, d):
        @pl.when(has_low)
        def _():
            lent_copy(kind, d, 0).start()

        @pl.when(has_up)
        def _():
            lent_copy(kind, d, 1).start()

    for d in range(3):
        far_copy(d).start()
    for d in range(3):
        mate_copy(d).start()
    greet(known.at[0])
    loads[0].wait()
    for side in range(2):
        ids = jnp.broadcast_to(send_ref[0, side:side + 1, :].astype(jnp.float32), (ghost, ghost)).T
        for at in range(nodes // 128):
            lanes = (lax.broadcasted_iota(jnp.int32, (ghost, 128), 1) + at * 128).astype(jnp.float32)
            lent_onehot[side * ghost:(side + 1) * ghost, at * 128:(at + 1) * 128] = jnp.where(
                ids == lanes, 1.0, 0.0).astype(jnp.bfloat16)
    for load in loads[1:]:
        load.wait()

    def own_rows(d, carry):
        lent_own[d] = jnp.dot(lent_onehot[...], basis_ref[d], preferred_element_type=jnp.float32).astype(jnp.bfloat16)
        wide[d, :nodes, pl.ds(lane_own, 128)] = basis_ref[d]
        return carry

    lax.fori_loop(0, 3, own_rows, 0)

    pl.semaphore_wait(known.at[0], greets)
    greet(known.at[1])
    for d in range(3):
        lend(0, d)
    pl.semaphore_wait(known.at[1], greets)
    greet(known.at[2])
    lend(2, 2)

    @pl.when(jnp.logical_not(has_low))
    def _():
        for d in range(3):
            wide[d, nodes:nodes + ghost, pl.ds(lane_half, 256)] = jnp.zeros((ghost, 256), jnp.bfloat16)

    @pl.when(jnp.logical_not(has_up))
    def _():
        for d in range(3):
            wide[d, nodes + ghost:, pl.ds(lane_half, 256)] = jnp.zeros((ghost, 256), jnp.bfloat16)

    for at, blk in enumerate((0, 2, 1, 3)):
        coef_s[:, at * 128:(at + 1) * 128] = coeffs_ref[:, blk * 128:(blk + 1) * 128]


    def build(i, carry):
        rows = pl.ds(pl.multiple_of(i * 64, 64), 64)
        ids = lax.broadcasted_iota(jnp.int32, (64, 128), 0) + i * 64
        for b in range(elems // 128):
            base = jnp.where(ids == connect_ref[b, 0:1, :], 1.0, 0.0)
            for t in range(3):
                one = jnp.where(ids == connect_ref[b, t + 1:t + 2, :], 1.0, 0.0)
                inc[rows, t * elems + b * 128:t * elems + (b + 1) * 128] = (one - base).astype(jnp.bfloat16)
        return carry

    lax.fori_loop(0, wide.shape[1] // 64, build, 0)

    def stage_far(d):
        far_copy(d).wait_recv()
        fwd_copy(d).start()

        @pl.when(d < 2)
        def _():
            lent_far[d] = jnp.dot(lent_onehot[...], wide[d, :nodes, pl.ds(lane_far, 128)],
                                  preferred_element_type=jnp.float32).astype(jnp.bfloat16)
            lend(1, d)

    def stage_rim(d):
        @pl.when(has_up)
        def _():
            lent_copy(0, d, 0).wait_recv()
            lent_copy(1, d, 0).wait_recv()

        @pl.when(has_low)
        def _():
            lent_copy(0, d, 1).wait_recv()
            lent_copy(1, d, 1).wait_recv()

        rim_copy(d).start()

    combos = coeffs_ref.shape[0]

    def stage_disp(d):
        mate_copy(d).wait_recv()
        fwd_copy(d).wait_recv()
        rim_copy(d).wait_recv()
        disp = lax.dot_general(coef_s[...], wide[d], (((1,), (1,)), ((), ())),
                               preferred_element_type=jnp.float32).astype(jnp.bfloat16)
        disp_s[...] = disp

        def expand(t, carry):
            lanes = pl.ds(pl.multiple_of(t * elems, 128), elems)
            disp_v[pl.ds(pl.multiple_of(d * combos, combos), combos), lanes] = jnp.dot(
                disp_s[...], inc[:, lanes], preferred_element_type=jnp.float32)
            return carry

        lax.fori_loop(0, 3, expand, 0, unroll=True)

    stage_far(0)
    pl.semaphore_wait(known.at[2], greets)

    def arrive(d, carry):
        @pl.when(d < 2)
        def _():
            stage_far(d + 1)
        stage_rim(d)
        stage_disp(d)
        return carry

    lax.fori_loop(0, 3, arrive, 0)

    count = count_ref[0]
    slots = wide.shape[1]
    modes = wide.shape[2]
    scale = (modes / (3.0 * nodes * n_mesh)) ** 0.5
    chunks = part_out.shape[0]
    crow = combos // chunks
    tile = 16

    def chunk(h, outer):
        def tile_force(i, carry):
            for b in range(elems // 128):
                lane = lax.broadcasted_iota(jnp.int32, (1, 128), 1) + b * 128
                k = jnp.where(lane < count, stiff_ref[b:b + 1, :], 0.0)
                k3 = jnp.broadcast_to(k * stiff_cubic, (tile, 128))
                kt = jnp.broadcast_to(k * twist_ratio, (tile, 128))
                kb = jnp.broadcast_to(k, (tile, 128))

                def vec(t):
                    return [disp_v[pl.ds(pl.multiple_of(h * crow + d * combos + i * tile, tile), tile),
                                   t * elems + b * 128:t * elems + (b + 1) * 128] for d in range(3)]
                vb, vc, vd = vec(0), vec(1), vec(2)

                def dot3(x, y):
                    return x[0] * y[0] + x[1] * y[1] + x[2] * y[2]

                def sub3(x, y):
                    return [x[j] - y[j] for j in range(3)]

                def stiff(x):
                    return kb + k3 * dot3(x, x)
                bc, cd, bd = sub3(vc, vb), sub3(vd, vc), sub3(vd, vb)
                sab, sac, sad = stiff(vb), stiff(vc), stiff(vd)
                sbc, scd, sbd = stiff(bc), stiff(cd), stiff(bd)
                for d in range(3):
                    tw = kt * (vb[d] + cd[d])
                    tbc, tcd, tbd = sbc * bc[d], scd * cd[d], sbd * bd[d]
                    fb = sab * vb[d] - tbc - tbd + tw
                    fc = sac * vc[d] + tbc - tcd - tw
                    fd = sad * vd[d] + tcd + tbd + tw
                    for t, f in enumerate((fb, fc, fd)):
                        high = f.astype(jnp.bfloat16)
                        low = (f - high.astype(jnp.float32)).astype(jnp.bfloat16)
                        lanes = slice(t * elems + b * 128, t * elems + (b + 1) * 128)
                        force_s[pl.ds(pl.multiple_of(d * crow + i * tile, tile), tile), lanes] = high
                        force_s[pl.ds(pl.multiple_of((3 + d) * crow + i * tile, tile), tile), lanes] = low
            return carry

        lax.fori_loop(0, crow // tile, tile_force, 0)

        modal_acc[...] = jnp.zeros_like(modal_acc)

        def scatter(g, carry):
            rows = pl.ds(pl.multiple_of(g * 256, 256), 256)
            both = lax.dot_general(force_s[...], inc[rows, :], (((1,), (1,)), ((), ())),
                                   preferred_element_type=jnp.float32)
            nodal = (both[:3 * crow] + both[3 * crow:]).astype(jnp.bfloat16)
            add = jnp.dot(nodal[:crow], wide[0, rows, :], preferred_element_type=jnp.float32)
            for d in range(1, 3):
                add += jnp.dot(nodal[d * crow:(d + 1) * crow], wide[d, rows, :], preferred_element_type=jnp.float32)
            modal_acc[...] += add
            return carry

        lax.fori_loop(0, slots // 256, scatter, 0, unroll=True)

        def encode(to, value):
            peak = jnp.maximum(jnp.max(jnp.abs(value), axis=0, keepdims=True), 1e-30)
            power = jnp.ceil(jnp.log2(peak))
            whole = jnp.round(value * (32000.0 * jnp.exp2(-power)))
            part_own[h, to] = value
            part_out[h, to, :crow // 2] = whole.astype(jnp.int32).astype(jnp.int16)
            part_out[h, to, crow // 2:] = jnp.broadcast_to(power, (16, 128)).astype(jnp.int32).astype(jnp.int16)

        low_half = lax.broadcasted_iota(jnp.int32, (crow // 2, 128), 1) < 64
        for blk in range(4):
            at = ((blk % 2) * 2 + blk // 2) * 128
            top = modal_acc[:crow // 2, at:at + 128] * scale
            bottom = modal_acc[crow // 2:, at:at + 128] * scale
            encode(2 * blk, jnp.where(low_half, top, pltpu.roll(bottom, 64, 1)))
            encode(2 * blk + 1, jnp.where(low_half, pltpu.roll(top, 64, 1), bottom))
        for r in range(1, n_mesh):
            part_copy(remote, part_out, part_in, s_part, r_part, h, r, p, q, n_mesh).start()
        return outer

    lax.fori_loop(0, chunks, chunk, 0)

    def collect(h, outer):
        total = part_own[h, p]
        for r in range(1, n_mesh):
            part_copy(remote, part_out, part_in, s_part, r_part, h, r, p, q, n_mesh).wait_recv()
            unit = jnp.exp2(part_in[h, r - 1, crow // 2:].astype(jnp.int32).astype(jnp.float32)[:1]) * (1.0 / 32000.0)
            total = total + part_in[h, r - 1, :crow // 2].astype(jnp.int32).astype(jnp.float32) * unit
        at = pl.multiple_of(h * crow, crow)
        out_ref[pl.ds(at, crow // 2), :] = total[:, :64]
        out_ref[pl.ds(at + crow // 2, crow // 2), :] = pltpu.roll(total, 64, 1)[:, :64]
        return outer

    lax.fori_loop(0, chunks, collect, 0)

    for d in range(3):
        far_copy(d).wait_send()
        mate_copy(d).wait_send()
        fwd_copy(d).wait_send()
        rim_copy(d).wait_send()
        for kind in range(2):
            @pl.when(has_low)
            def _():
                lent_copy(kind, d, 0).wait_send()

            @pl.when(has_up)
            def _():
                lent_copy(kind, d, 1).wait_send()
    for h in range(chunks):
        for r in range(1, n_mesh):
            part_copy(remote, part_out, part_in, s_part, r_part, h, r, p, q, n_mesh).wait_send()


def part_copy(remote, part_out, part_in, s_part, r_part, h, r, p, q, n_mesh):
    to = lax.rem(p + r, n_mesh)
    return remote(part_out.at[h, to], part_in.at[h, r - 1], s_part.at[h, r - 1], r_part.at[h, r - 1], to, q)


def fused_body(coeffs, basis, connect, stiffness, send_lists, elem_count):
    n_mesh = lax.axis_size("mesh")
    combos, modes = coeffs.shape
    nodes = basis.shape[1]
    ghost = send_lists.shape[2]
    slots = nodes + 2 * ghost
    elems = stiffness.shape[0] * 128
    chunks = 2
    crow = combos // chunks
    bf16, f32 = jnp.bfloat16, jnp.float32
    vmem = pl.BlockSpec(memory_space=pltpu.VMEM)
    dma = pltpu.SemaphoreType.DMA
    return pl.pallas_call(
        functools.partial(fused_kernel, n_mesh),
        out_shape=jax.ShapeDtypeStruct((combos, modes // n_mesh), f32),
        in_specs=[pl.BlockSpec(memory_space=pl.ANY)] * 5 + [pl.BlockSpec(memory_space=pltpu.SMEM)],
        out_specs=vmem,
        scratch_shapes=[
            pltpu.VMEM(coeffs.shape, bf16),
            pltpu.VMEM(basis.shape, bf16),
            pltpu.VMEM(connect.shape, jnp.int32),
            pltpu.VMEM(stiffness.shape, f32),
            pltpu.VMEM(send_lists.shape, jnp.int32),
            dma((5,)), pltpu.SemaphoreType.REGULAR((3,)),
            pltpu.VMEM((combos, modes), bf16),
            pltpu.VMEM((3, slots, modes), bf16),
            pltpu.VMEM((slots, 3 * elems), bf16),
            pltpu.VMEM((2 * ghost, nodes), bf16),
            pltpu.VMEM((3, 2 * ghost, 128), bf16),
            pltpu.VMEM((3, 2 * ghost, 128), bf16),
            pltpu.VMEM((3 * combos, 3 * elems), f32),
            pltpu.VMEM((6 * crow, 3 * elems), bf16),
            pltpu.VMEM((crow, modes), f32),
            pltpu.VMEM((combos, slots), bf16),
            pltpu.VMEM((chunks, n_mesh, crow // 2, 128), f32),
            pltpu.VMEM((chunks, n_mesh, crow // 2 + 16, 128), jnp.int16),
            pltpu.VMEM((chunks, n_mesh - 1, crow // 2 + 16, 128), jnp.int16),
            dma((3,)), dma((3,)), dma((3,)), dma((3,)), dma((3,)), dma((3,)),
            dma((2, 3, 2)), dma((2, 3, 2)), dma((3,)), dma((3,)),
            dma((chunks, n_mesh - 1)), dma((chunks, n_mesh - 1)),
        ],
        compiler_params=pltpu.CompilerParams(
            collective_id=0, has_side_effects=True, vmem_limit_bytes=48 * 2 ** 20),
        cost_estimate=pl.CostEstimate(flops=6 * 10 ** 9, bytes_accessed=4 * 10 ** 6, transcendentals=0),
    )(coeffs, basis, connect, stiffness, send_lists, elem_count)


def any_body(coeffs, basis, connect, stiffness, send_lists, elem_count):
    fits = (lax.axis_size("comb") == 4 and lax.axis_size("mesh") == 8 and coeffs.shape == (256, 512)
            and basis.shape == (3, 512, 128) and send_lists.shape[1:] == (2, 128) and stiffness.shape[0] == 4)
    return (fused_body if fits else body)(coeffs, basis, connect, stiffness, send_lists, elem_count)


def solution(mesh):
    in_specs = (
        P("comb", None),
        P(None, "mesh", "comb"),
        P("mesh", None, None),
        P("mesh", None),
        P("mesh", None, None),
        P("mesh"),
    )
    out_specs = P("comb", "mesh")
    return jax.shard_map(any_body, mesh=mesh, in_specs=in_specs, out_specs=out_specs, check_vma=False)
```
